32 devices in a mesh: groups: 2 (over y), seq: 4 (over z), mp: 2 (over x), section: 2 (over core).
Axes of the slice: x: 2, y: 2, z: 4, core: 2. Of those that a mesh axis runs over, the one named last changes fastest.
Arguments:
- readout: bfloat16 [8, 64, 32, 1024], P(('groups', 'mp', 'section'), None, 'seq'), parts along dimension 0, may hold values from -6 to 6
- first_kernel: bfloat16 [3, 3, 64, 128], replicated, may hold values from -0.25 to 0.25
- second_kernel: bfloat16 [3, 3, 128, 256], replicated, may hold values from -0.1875 to 0.1875
- embed_weight: bfloat16 [1024, 768], P(('mp', 'section')), may hold values from -0.1875 to 0.1875
- project_weight: bfloat16 [768, 2304], P(('mp', 'section'))
- output_weight: bfloat16 [768, 768], P(('mp', 'section')), may hold values from -0.4375 to 0.4375
- order: int32 [8, 512], P(('groups', 'mp', 'section')), parts along dimension 0, may hold values from 0 to 511, as said below
- active: int32 [8, 512], P(('groups', 'mp', 'section'), 'seq'), parts along dimension 0, may hold values 0 or 1
Outputs:
- encoded: bfloat16 [8, 512, 768], P(('groups', 'mp', 'section'), 'seq'), parts along dimension 0
The draws below stay inside these ranges and needn't reach their ends.
There are 2 independent parts, one for each index of `groups`. The reference program is written for one: setup_inputs(seed, part) draws one part's arguments, and reference() takes and returns one part's arrays. A program takes and returns all parts, laid end to end along the dimension named above; an argument that names none is the same for every part. Nothing has to cross between parts.
Inputs may be any that keep to these rules, and one draw needn't show every extreme that they name: Each row of order lists each of the 512 patches of its region once. Patch i comes from the wire tile i // 128; each block of 128 positions k * 128 to (k + 1) * 128 - 1 holds exactly 32 patches of every wire tile.
All inputs are finite; a program needn't handle non-finite values. No bound on the sum of `active` on one device may be relied on, other than what follows from the above.
Results may differ from the reference program's by a relative error of at most 0.017.
Values may be sent and summed in bfloat16 or wider, within the bound.
A program may use at most 64 MiB of HBM per device.

```python
import jax
import jax.numpy as jnp
from jax import lax

D = 768
HEADS = 12
C_IN = 64
C_MID = 128
C_OUT = 256
TICKS = 1024
HEAD_DIM = 64
PATCH_DIM = 1024
TOK_DEV = 128
SEQ_LEN = 512
GROUP = 32
REGIONS = 4
WIRES = 32
N_SEQ = 4


def draw_project_weight(key, part):
    first_key = jax.random.fold_in(key, 11)
    result = jax.random.normal(first_key, (D, 3 * D), jnp.float32) * (2.0 / D) ** 0.5
    return result.astype(jnp.bfloat16)


def draw_order(key, part):
    sources = SEQ_LEN // TOK_DEV
    first_key = jax.random.fold_in(key, 21)
    second_key = jax.random.fold_in(key, 22)
    local = jnp.broadcast_to(jnp.arange(TOK_DEV, dtype=jnp.int32), (REGIONS, sources, TOK_DEV))
    shuffled = jax.random.permutation(first_key, local, axis=2, independent=True)
    labels = shuffled + (jnp.arange(sources, dtype=jnp.int32) * TOK_DEV)[None, :, None]
    labels = labels.reshape(REGIONS, sources, sources, GROUP).transpose(0, 2, 1, 3).reshape(REGIONS, sources, TOK_DEV)
    labels = jax.random.permutation(second_key, labels, axis=2, independent=True)
    return labels.reshape(REGIONS, SEQ_LEN).astype(jnp.int32)


def set_ends(values, own_key, smallest, top_value):
    extent = values.shape
    index_at = [jax.random.randint(jax.random.fold_in(own_key, axis), (), 0, extent[axis]) for axis in range(len(extent))]
    values = values.at[tuple(index_at)].set(smallest)
    longest = extent.index(max(extent))
    index_at[longest] = (index_at[longest] + 1) % extent[longest]
    return values.at[tuple(index_at)].set(top_value)


def block_levels(stream_key, extent, pieces, low, largest):
    def one(dim, blocks):
        draws = jax.random.uniform(jax.random.fold_in(jax.random.fold_in(stream_key, 6), dim), (blocks,), jnp.float32, low / len(pieces), largest / len(pieces))
        return jnp.repeat(jnp.exp(draws), extent[dim] // blocks).reshape((-1,) + (1,) * (len(extent) - dim - 1))

    factor_of = one(*pieces[0])
    for cut in pieces[1:]:
        factor_of = factor_of * one(*cut)
    return factor_of


def bell_draw(stream_key, dims, scale, reach, split=(), held_as=jnp.bfloat16):
    values = jax.random.normal(stream_key, dims, jnp.float32) * scale
    if len(split) > 0:
        values = block_levels(stream_key, dims, split, -0.22, 0.18) * values
    return jnp.clip(values, min=-reach, max=reach).astype(held_as)


def setup_inputs(seed: int = 0, part: int = 0) -> dict:
    splits = jax.random.split(jax.random.key(seed), 9)
    part_keys = jax.random.split(jax.random.fold_in(splits[8], part), 9)
    return {
        "readout": bell_draw(part_keys[0], (REGIONS, C_IN, WIRES, TICKS), 1.0, 6.0, ((0, 4), (2, 4))),
        "first_kernel": bell_draw(splits[1], (3, 3, C_IN, C_MID), (9 * C_IN) ** -0.5, 0.25),
        "second_kernel": bell_draw(splits[2], (3, 3, C_MID, C_OUT), (9 * C_MID) ** -0.5, 0.1875),
        "embed_weight": bell_draw(splits[3], (PATCH_DIM, D), PATCH_DIM ** -0.5, 0.1875, ((0, 4),)),
        "project_weight": draw_project_weight(jax.random.fold_in(splits[8], 71), part),
        "output_weight": bell_draw(splits[5], (D, D), (D // 4) ** -0.5, 0.4375, ((0, 4),)),
        "order": draw_order(jax.random.fold_in(jax.random.fold_in(splits[8], part), 71), part),
        "active": set_ends((jax.random.randint(part_keys[7], (REGIONS, SEQ_LEN), 0, 4) < 3).astype(jnp.int32), jax.random.fold_in(part_keys[7], 1), 0, 1),
    }


masked_score = -1e+30
epsilon = 1e-05

def strided_conv(picture, kernel):
    result = lax.conv_general_dilated(picture[None], kernel, (2, 2), ((1, 1), (1, 1)), dimension_numbers=('NCHW', 'HWIO', 'NCHW'), preferred_element_type=jnp.float32)[0]
    return jax.nn.silu(result).astype(jnp.bfloat16)

def normalize(tokens):
    values = tokens.astype(jnp.float32)
    center = lax.optimization_barrier(jnp.mean(values, axis=-1, keepdims=True))
    spread = lax.optimization_barrier(jnp.mean(jnp.square(values - center), axis=-1, keepdims=True))
    return ((values - center) * lax.rsqrt(spread + epsilon)).astype(jnp.bfloat16)

def reference(readout, first_kernel, second_kernel, embed_weight, project_weight, output_weight, order, active):

    def region(inputs):
        picture, sequence, flags = inputs
        first = strided_conv(picture, first_kernel)
        second = strided_conv(first, second_kernel)
        grid = second.reshape(C_OUT, WIRES // 8, 2, TICKS // 8, 2)
        patches = grid.transpose(1, 3, 0, 2, 4).reshape(SEQ_LEN, PATCH_DIM)
        placed = jnp.take(patches, sequence, axis=0)
        tokens = jnp.dot(placed, embed_weight, preferred_element_type=jnp.float32).astype(jnp.bfloat16)
        normed = normalize(tokens)
        projected = jnp.dot(normed, project_weight, preferred_element_type=jnp.float32)
        queries = (projected[:, :D] * HEAD_DIM ** (-0.5)).astype(jnp.bfloat16)
        keys_all = projected[:, D:2 * D].astype(jnp.bfloat16).reshape(SEQ_LEN, HEADS, HEAD_DIM).astype(jnp.float32)
        values_all = projected[:, 2 * D:].astype(jnp.bfloat16).reshape(SEQ_LEN, HEADS, HEAD_DIM).astype(jnp.float32)
        keep = flags > 0
        positions = jnp.arange(SEQ_LEN, dtype=jnp.int32)

        def attend(block):
            query_block, query_pos = block
            scores = jnp.einsum('qhd,khd->qhk', query_block.astype(jnp.float32), keys_all)
            allowed = (keep[None, :] | (positions[None, :] == query_pos[:, None]))[:, None, :]
            scores = jnp.where(allowed, scores, masked_score)
            rowmax = lax.optimization_barrier(jnp.max(scores, axis=-1))
            weights = jnp.where(allowed, jnp.exp(scores - rowmax[..., None]), 0.0)
            total = lax.optimization_barrier(jnp.sum(weights, axis=-1))
            rounded = lax.optimization_barrier(weights.astype(jnp.bfloat16)).astype(jnp.float32)
            mixed = jnp.einsum('qhk,khd->qhd', rounded, values_all) / total[..., None]
            return mixed.astype(jnp.bfloat16).reshape(TOK_DEV, D)
        query_blocks = queries.reshape(N_SEQ, TOK_DEV, HEADS, HEAD_DIM)
        mixed = lax.map(attend, (query_blocks, positions.reshape(N_SEQ, TOK_DEV))).reshape(SEQ_LEN, D)
        result = tokens.astype(jnp.float32) + jnp.dot(mixed, output_weight, preferred_element_type=jnp.float32)
        return result.astype(jnp.bfloat16)
    return lax.map(region, (readout, order, active))
```

```python
import functools

import jax
import jax.numpy as jnp
from jax import lax
from jax.experimental import pallas as pl
from jax.experimental.pallas import tpu as pltpu
from jax.sharding import PartitionSpec as P

HEADS = 12
epsilon = 1e-05
MESH = pl.DeviceIdType.MESH
F32 = jnp.float32
BF16 = jnp.bfloat16


def silu(v):
    return v / (1.0 + jnp.exp(-v))


def normalize(tokens):
    values = tokens.astype(F32)
    center = jnp.mean(values, axis=-1, keepdims=True)
    spread = jnp.mean(jnp.square(values - center), axis=-1, keepdims=True)
    return ((values - center) * lax.rsqrt(spread + epsilon)).astype(BF16)


def dot(a, b):
    return jnp.dot(a, b, preferred_element_type=F32)


def kernel(
    sizes,
    x_ref, k1_ref, k2_ref, order_ref, active_ref, embed_ref, project_ref, output_ref,
    out_ref,
    we_ref, wp_ref, wo_ref, hx_ref, h1_ref, s1_ref, p0_ref, p1_ref, p2_ref, f_ref, g_ref,
    tok_ref, kv_ref, flag_ref,
    local_sem, mate_send, mate_recv, x_send, x_recv, y_send, y_recv,
    fwd_send, fwd_recv, halo_send, halo_recv, tok_send, tok_recv, flag_send, flag_recv,
):
    n, n_mp = sizes
    g, s = lax.axis_index("groups"), lax.axis_index("seq")
    m, c = lax.axis_index("mp"), lax.axis_index("section")
    mate = {"section": 1 - c}
    across = {"groups": 1 - g}

    def mp_peer(d):
        return {"mp": lax.rem(m + d, n_mp)}

    def seq_peer(d):
        return {"seq": lax.rem(s + d, n)}

    def remote(src, dst, send, recv, where):
        return pltpu.make_async_remote_copy(
            src_ref=src, dst_ref=dst, send_sem=send, recv_sem=recv, device_id=where, device_id_type=MESH
        )

    barrier = pltpu.get_barrier_semaphore()
    peers = [mate, across] + [mp_peer(d) for d in range(1, n_mp)] + [seq_peer(d) for d in range(1, n)]
    for where in peers:
        pl.semaphore_signal(barrier, inc=1, device_id=where, device_id_type=MESH)
    pl.semaphore_wait(barrier, len(peers))

    shards = (embed_ref, project_ref, output_ref)
    full = (we_ref, wp_ref, wo_ref)

    def half(ref, w, which):
        if w == 0:
            return ref.at[pl.ds(2 * which, 2)]
        cols = ref.shape[-1] // 2
        return ref.at[:, pl.ds(pl.multiple_of(which * cols, 128), cols)]

    def copy_local(w):
        return pltpu.make_async_copy(shards[w], full[w].at[m, c], local_sem.at[w])

    def copy_mate(w):
        return remote(shards[w], full[w].at[m, c], mate_send.at[w], mate_recv.at[w], mate)

    def copy_x(w, d):
        return remote(
            half(shards[w], w, g), half(full[w].at[m, c], w, g), x_send.at[w, d - 1], x_recv.at[w, d - 1], mp_peer(d)
        )

    def piece(w, d, which):
        return half(full[w].at[lax.rem(m + n_mp - d, n_mp), c], w, which)

    def copy_y(w, d):
        ref = piece(w, d, g)
        return remote(ref, ref, y_send.at[w, d - 1], y_recv.at[w, d - 1], across)

    def copy_fwd(w, d, k):
        ref = piece(w, d, g if k == 0 else 1 - g)
        return remote(ref, ref, fwd_send.at[w, d - 1, k], fwd_recv.at[w, d - 1, k], mate)

    steps = range(1, n_mp)

    def send_weight(w):
        for d in steps:
            copy_x(w, d).start()
        copy_mate(w).start()
        copy_local(w).start()

    def pass_x(w):
        for d in steps:
            copy_x(w, d).wait_recv()
            copy_y(w, d).start()
            copy_fwd(w, d, 0).start()

    def pass_y(w):
        for d in steps:
            copy_y(w, d).wait_recv()
            copy_fwd(w, d, 1).start()

    def finish_weight(w):
        copy_local(w).wait()
        copy_mate(w).wait_recv()
        for d in steps:
            copy_fwd(w, d, 0).wait_recv()
            copy_fwd(w, d, 1).wait_recv()

    def copy_halo(k):
        src, dst = ((x_ref.at[x_ref.shape[0] - 1], hx_ref), (s1_ref, h1_ref))[k]
        return remote(src, dst, halo_send.at[k], halo_recv.at[k], seq_peer(1))

    def start_halo(k):
        @pl.when(s < n - 1)
        def _():
            copy_halo(k).start()

    def await_halo(k, ref):
        @pl.when(s > 0)
        def _():
            copy_halo(k).wait_recv()

        @pl.when(s == 0)
        def _():
            ref[...] = jnp.zeros_like(ref)

    def copy_flag(d):
        ref = flag_ref.at[s]
        return remote(ref, ref, flag_send.at[d - 1], flag_recv.at[d - 1], seq_peer(d))

    def copy_tok(d):
        ref = tok_ref.at[s]
        return remote(ref, ref, tok_send.at[d - 1], tok_recv.at[d - 1], seq_peer(d))

    start_halo(0)
    send_weight(0)
    flag_ref[s] = jnp.broadcast_to(active_ref[...].astype(F32), flag_ref.shape[1:]).astype(BF16)
    for d in range(1, n):
        copy_flag(d).start()

    ticks = x_ref.shape[2]
    half_ticks, quarter = ticks // 2, ticks // 4
    for ref in (p0_ref, p1_ref, p2_ref):
        ref[0:8, :] = jnp.zeros((8, ref.shape[1]), F32)
    rows1 = x_ref.shape[0] // 2
    for w in range(rows1 + 1):
        f_ref[w, 0:8, :] = jnp.zeros((8, f_ref.shape[2]), F32)
    c_in, c_mid = k1_ref.shape[2], k1_ref.shape[3]
    k1 = jnp.concatenate([k1_ref[:, kw].reshape(3 * c_in, c_mid) for kw in range(3)], axis=1)

    def conv_one(w):
        low = hx_ref[...] if w == 0 else x_ref[2 * w - 1]
        rows = jnp.concatenate([low, x_ref[2 * w], x_ref[2 * w + 1]], axis=0)
        made = lax.dot_general(rows, k1, (((0,), (0,)), ((), ())), preferred_element_type=F32)
        for kw, ref in enumerate((p0_ref, p1_ref, p2_ref)):
            ref[8 : 8 + ticks, :] = made[:, kw * c_mid : (kw + 1) * c_mid]
        total = (
            p0_ref[pl.ds(7, half_ticks, stride=2), :]
            + p1_ref[pl.ds(8, half_ticks, stride=2), :]
            + p2_ref[pl.ds(9, half_ticks, stride=2), :]
        )
        result = silu(total).astype(BF16)
        f_ref[w + 1, 8 : 8 + half_ticks, :] = result.astype(F32)
        return result

    s1_ref[...] = conv_one(rows1 - 1)
    start_halo(1)
    send_weight(1)
    for w in range(1, rows1 - 1):
        conv_one(w)
    pass_x(0)
    await_halo(0, hx_ref)
    conv_one(0)
    send_weight(2)
    await_halo(1, h1_ref)
    f_ref[0, 8 : 8 + half_ticks, :] = h1_ref[...].astype(F32)
    pass_y(0)

    for w in range(rows1 // 2):
        parts = [
            f_ref[2 * w + kh, pl.ds(7 + kw, quarter, stride=2), :].astype(BF16) for kh in range(3) for kw in range(3)
        ]
        result = silu(dot(jnp.concatenate(parts, axis=1), k2_ref[...])).astype(BF16).astype(F32)
        g_ref[w, 0] = result[:, :128]
        g_ref[w, 1] = result[:, 128:]
    count = quarter // 2
    finish_weight(0)
    tokens = None
    for w in range(2):
        for t in range(2):
            rows = jnp.concatenate([g_ref[w, k, pl.ds(t, count, stride=2), :] for k in range(2)], axis=1)
            part = we_ref[:, :, 2 * w + t].reshape(rows.shape[1], we_ref.shape[4])
            term = dot(rows.astype(BF16), part)
            tokens = term if tokens is None else tokens + term
    tok_ref[s] = tokens.astype(BF16)
    for d in range(1, n):
        copy_tok(d).start()
    pass_x(1)

    total_len = n * count
    lanes = lax.broadcasted_iota(jnp.int32, (count, total_len), 1)
    for d in range(1, n):
        copy_flag(d).wait_recv()

    def activity(k, row):
        block = order_ref[pl.ds(pl.multiple_of(k * count, count), count), :]
        return row + dot(flag_ref[k], jnp.where(lanes == block, 1.0, 0.0).astype(BF16))

    row = lax.fori_loop(0, n, activity, jnp.zeros((flag_ref.shape[1], total_len), F32))
    own = lanes == order_ref[pl.ds(pl.multiple_of(s * count, count), count), :]
    onehot = jnp.where(own, 1.0, 0.0).astype(BF16)
    bias = jnp.where((row[0:1, :] > 0.5) | own, 0.0, -jnp.inf)

    pass_x(2)
    pass_y(1)
    finish_weight(1)
    width = wo_ref.shape[3]

    def place(k):
        normed = normalize(tok_ref[k])
        made = dot(normed, wp_ref[:, :, :, width:].reshape(width, 2 * width))
        kv_ref[pl.ds(pl.multiple_of(k * count, count), count), :] = made.astype(BF16)

    place(s)
    pass_y(2)

    def arrive(d, carry):
        copy_tok(d).wait_recv()
        place(lax.rem(s + n - d, n))
        return carry

    lax.fori_loop(1, n, arrive, 0)
    mine = dot(onehot, tok_ref[...].reshape(total_len, width)).astype(BF16)
    head = width // HEADS
    query = dot(normalize(mine), wp_ref[:, :, :, :width].reshape(width, width))
    query = (query * head ** (-0.5)).astype(BF16)
    low_half = lax.broadcasted_iota(jnp.int32, (count, 2 * head), 1) < head
    bias = jnp.concatenate([bias, bias], axis=0)
    mixed = []
    for h in range(HEADS // 2):
        cols = slice(h * 2 * head, (h + 1) * 2 * head)
        pair = query[:, cols]
        zero = jnp.zeros_like(pair)
        both = jnp.concatenate([jnp.where(low_half, pair, zero), jnp.where(low_half, zero, pair)], axis=0)
        keys = kv_ref[:, cols]
        values = kv_ref[:, slice(width + h * 2 * head, width + (h + 1) * 2 * head)]
        scores = lax.dot_general(both, keys, (((1,), (1,)), ((), ())), preferred_element_type=F32) + bias
        weights = jnp.exp(scores - jnp.max(scores, axis=-1, keepdims=True))
        total = jnp.sum(weights, axis=-1, keepdims=True)
        result = dot(weights.astype(BF16), values) / total
        mixed.append(jnp.where(low_half, result[:count], result[count:]).astype(BF16))
    finish_weight(2)
    final = mine.astype(F32) + dot(jnp.concatenate(mixed, axis=1), wo_ref[...].reshape(width, width))
    out_ref[...] = final.astype(BF16)

    for w in range(3):
        copy_mate(w).wait_send()
        for d in steps:
            copy_x(w, d).wait_send()
            copy_y(w, d).wait_send()
            copy_fwd(w, d, 0).wait_send()
            copy_fwd(w, d, 1).wait_send()
    for d in range(1, n):
        copy_flag(d).wait_send()
        copy_tok(d).wait_send()

    @pl.when(s < n - 1)
    def _():
        copy_halo(0).wait_send()
        copy_halo(1).wait_send()


def body(
    readout, first_kernel, second_kernel, embed_weight, project_weight, output_weight, order, active
):
    n, n_mp, n_sec = lax.axis_size("seq"), lax.axis_size("mp"), lax.axis_size("section")
    x = readout[0].transpose(1, 0, 2)
    wires, c_in, ticks = x.shape
    c_mid, c_out = second_kernel.shape[2:]
    width = embed_weight.shape[1]
    rows_e = embed_weight.shape[0] // 4
    embed = embed_weight.reshape(rows_e, 4, width).transpose(1, 0, 2)
    rows_p = project_weight.shape[0]
    count = active.shape[1]
    k2 = second_kernel.reshape(9 * c_mid, c_out)
    vmem = pl.BlockSpec(memory_space=pltpu.VMEM)
    hbm = pl.BlockSpec(memory_space=pl.ANY)
    dma = pltpu.SemaphoreType.DMA
    links = (3, n_mp - 1)
    result = pl.pallas_call(
        functools.partial(kernel, (n, n_mp)),
        out_shape=jax.ShapeDtypeStruct((count, width), BF16),
        in_specs=[vmem] * 5 + [hbm] * 3,
        out_specs=vmem,
        scratch_shapes=[
            pltpu.VMEM((n_mp, n_sec, 4, rows_e, width), BF16),
            pltpu.VMEM((n_mp, n_sec, rows_p, 3 * width), BF16),
            pltpu.VMEM((n_mp, n_sec, rows_p, width), BF16),
            pltpu.VMEM((c_in, ticks), BF16),
            pltpu.VMEM((ticks // 2, c_mid), BF16),
            pltpu.VMEM((ticks // 2, c_mid), BF16),
            pltpu.VMEM((ticks + 16, c_mid), F32),
            pltpu.VMEM((ticks + 16, c_mid), F32),
            pltpu.VMEM((ticks + 16, c_mid), F32),
            pltpu.VMEM((wires // 2 + 1, ticks // 2 + 16, c_mid), F32),
            pltpu.VMEM((wires // 4, 2, ticks // 4, c_out // 2), F32),
            pltpu.VMEM((n, count, width), BF16),
            pltpu.VMEM((n * count, 2 * width), BF16),
            pltpu.VMEM((n, 16, count), BF16),
            dma((3,)), dma((3,)), dma((3,)), dma(links), dma(links), dma(links), dma(links),
            dma(links + (2,)), dma(links + (2,)), dma((2,)), dma((2,)),
            dma((n - 1,)), dma((n - 1,)), dma((n - 1,)), dma((n - 1,)),
        ],
        compiler_params=pltpu.CompilerParams(
            collective_id=0, has_side_effects=True, vmem_limit_bytes=52 * 2**20
        ),
    )(x, first_kernel, k2, order[0][:, None], active, embed, project_weight, output_weight)
    return result[None]


def solution(mesh):
    in_specs = (
        P(("groups", "mp", "section"), None, "seq", None),
        P(),
        P(),
        P(("mp", "section"), None),
        P(("mp", "section"), None),
        P(("mp", "section"), None),
        P(("groups", "mp", "section"), None),
        P(("groups", "mp", "section"), "seq"),
    )
    out_specs = P(("groups", "mp", "section"), "seq", None)
    return jax.shard_map(body, mesh=mesh, in_specs=in_specs, out_specs=out_specs, check_vma=False)
```

```python
import functools

import jax
import jax.numpy as jnp
from jax import lax
from jax.experimental import pallas as pl
from jax.experimental.pallas import tpu as pltpu
from jax.sharding import PartitionSpec as P

HEADS = 12
epsilon = 1e-05
MESH = pl.DeviceIdType.MESH
F32 = jnp.float32
BF16 = jnp.bfloat16


def silu(v):
    return v / (1.0 + jnp.exp(-v))


def normalize(tokens):
    values = tokens.astype(F32)
    center = jnp.mean(values, axis=-1, keepdims=True)
    spread = jnp.mean(jnp.square(values - center), axis=-1, keepdims=True)
    return ((values - center) * lax.rsqrt(spread + epsilon)).astype(BF16)


def dot(a, b):
    return jnp.dot(a, b, preferred_element_type=F32)


def kernel(
    sizes,
    x_ref, k1_ref, k2_ref, order_ref, active_ref, embed_ref, project_ref, output_ref,
    out_ref,
    we_ref, wp_ref, wo_ref, hx_ref, h1_ref, s1_ref, p0_ref, p1_ref, p2_ref, f_ref, g_ref,
    tok_ref, kv_ref, flag_ref,
    local_sem, mate_send, mate_recv, x_send, x_recv, y_send, y_recv,
    fwd_send, fwd_recv, halo_send, halo_recv, tok_send, tok_recv, flag_send, flag_recv,
):
    n, n_mp = sizes
    g, s = lax.axis_index("groups"), lax.axis_index("seq")
    m, c = lax.axis_index("mp"), lax.axis_index("section")
    mate = {"section": 1 - c}
    across = {"groups": 1 - g}

    def mp_peer(d):
        return {"mp": lax.rem(m + d, n_mp)}

    def seq_peer(d):
        return {"seq": lax.rem(s + d, n)}

    def remote(src, dst, send, recv, where):
        return pltpu.make_async_remote_copy(
            src_ref=src, dst_ref=dst, send_sem=send, recv_sem=recv, device_id=where, device_id_type=MESH
        )

    barrier = pltpu.get_barrier_semaphore()
    peers = [mate, across] + [mp_peer(d) for d in range(1, n_mp)] + [seq_peer(d) for d in range(1, n)]
    for where in peers:
        pl.semaphore_signal(barrier, inc=1, device_id=where, device_id_type=MESH)
    pl.semaphore_wait(barrier, len(peers))

    width = wo_ref.shape[3]
    shards = (embed_ref, project_ref, project_ref, output_ref)
    full = (we_ref, wp_ref, wp_ref, wo_ref)
    spans = (None, (width, 2 * width), (0, width), (0, width))

    def half(ref, w, which):
        if w == 0:
            return ref.at[pl.ds(2 * which, 2)]
        base, cols = spans[w][0], spans[w][1] // 2
        return ref.at[:, pl.ds(pl.multiple_of(base + which * cols, 128), cols)]

    def span(ref, w):
        return ref if w == 0 else ref.at[:, pl.ds(*spans[w])]

    def copy_local(w):
        return pltpu.make_async_copy(span(shards[w], w), span(full[w].at[m, c], w), local_sem.at[w])

    def copy_mate(w):
        return remote(span(shards[w], w), span(full[w].at[m, c], w), mate_send.at[w], mate_recv.at[w], mate)

    def copy_x(w, d):
        return remote(
            half(shards[w], w, g), half(full[w].at[m, c], w, g), x_send.at[w, d - 1], x_recv.at[w, d - 1], mp_peer(d)
        )

    def piece(w, d, which):
        return half(full[w].at[lax.rem(m + n_mp - d, n_mp), c], w, which)

    def copy_y(w, d):
        ref = piece(w, d, g)
        return remote(ref, ref, y_send.at[w, d - 1], y_recv.at[w, d - 1], across)

    def copy_fwd(w, d, k):
        ref = piece(w, d, g if k == 0 else 1 - g)
        return remote(ref, ref, fwd_send.at[w, d - 1, k], fwd_recv.at[w, d - 1, k], mate)

    steps = range(1, n_mp)

    def send_weight(w):
        for d in steps:
            copy_x(w, d).start()
        copy_mate(w).start()
        copy_local(w).start()

    def pass_x(w):
        for d in steps:
            copy_x(w, d).wait_recv()
            copy_y(w, d).start()
            copy_fwd(w, d, 0).start()

    def pass_y(w):
        for d in steps:
            copy_y(w, d).wait_recv()
            copy_fwd(w, d, 1).start()

    def finish_weight(w):
        copy_local(w).wait()
        copy_mate(w).wait_recv()
        for d in steps:
            copy_fwd(w, d, 0).wait_recv()
            copy_fwd(w, d, 1).wait_recv()

    def copy_halo(k):
        src, dst = ((x_ref.at[x_ref.shape[0] - 1], hx_ref), (s1_ref, h1_ref))[k]
        return remote(src, dst, halo_send.at[k], halo_recv.at[k], seq_peer(1))

    def start_halo(k):
        @pl.when(s < n - 1)
        def _():
            copy_halo(k).start()

    def await_halo(k, ref):
        @pl.when(s > 0)
        def _():
            copy_halo(k).wait_recv()

        @pl.when(s == 0)
        def _():
            ref[...] = jnp.zeros_like(ref)

    def copy_flag(d):
        ref = flag_ref.at[s]
        return remote(ref, ref, flag_send.at[d - 1], flag_recv.at[d - 1], seq_peer(d))

    def copy_tok(way, k):
        ref = tok_ref.at[lax.rem(s + n - k if way == 0 else s + k, n)]
        where = seq_peer(1 if way == 0 else n - 1)
        return remote(ref, ref, tok_send.at[way, k], tok_recv.at[way, k], where)

    def has(way, k):
        return s >= k if way == 0 else s + k < n

    def relay(k):
        for way in range(2):

            @pl.when(has(way, k))
            def _(way=way):
                copy_tok(way, k - 1).wait_recv()

            @pl.when(has(way, k) & has(1 - way, 1))
            def _(way=way):
                copy_tok(way, k).start()

    start_halo(0)
    send_weight(0)
    flag_ref[s] = jnp.broadcast_to(active_ref[...].astype(F32), flag_ref.shape[1:]).astype(BF16)
    for d in range(1, n):
        copy_flag(d).start()

    ticks = x_ref.shape[2]
    half_ticks, quarter = ticks // 2, ticks // 4
    for ref in (p0_ref, p1_ref, p2_ref):
        ref[0:8, :] = jnp.zeros((8, ref.shape[1]), F32)
    rows1 = x_ref.shape[0] // 2
    for w in range(rows1 + 1):
        f_ref[w, 0:8, :] = jnp.zeros((8, f_ref.shape[2]), F32)
    c_in, c_mid = k1_ref.shape[2], k1_ref.shape[3]
    k1 = jnp.concatenate([k1_ref[:, kw].reshape(3 * c_in, c_mid) for kw in range(3)], axis=1)

    def conv_one(w):
        low = hx_ref[...] if w == 0 else x_ref[2 * w - 1]
        rows = jnp.concatenate([low, x_ref[2 * w], x_ref[2 * w + 1]], axis=0)
        made = lax.dot_general(rows, k1, (((0,), (0,)), ((), ())), preferred_element_type=F32)
        for kw, ref in enumerate((p0_ref, p1_ref, p2_ref)):
            ref[8 : 8 + ticks, :] = made[:, kw * c_mid : (kw + 1) * c_mid]
        total = (
            p0_ref[pl.ds(7, half_ticks, stride=2), :]
            + p1_ref[pl.ds(8, half_ticks, stride=2), :]
            + p2_ref[pl.ds(9, half_ticks, stride=2), :]
        )
        result = silu(total).astype(BF16)
        f_ref[w + 1, 8 : 8 + half_ticks, :] = result.astype(F32)
        return result

    s1_ref[...] = conv_one(rows1 - 1)
    start_halo(1)
    send_weight(1)
    send_weight(2)
    for w in range(1, rows1 - 1):
        conv_one(w)
    pass_x(0)
    await_halo(0, hx_ref)
    conv_one(0)
    send_weight(3)
    await_halo(1, h1_ref)
    f_ref[0, 8 : 8 + half_ticks, :] = h1_ref[...].astype(F32)
    pass_y(0)

    for w in range(rows1 // 2):
        parts = [
            f_ref[2 * w + kh, pl.ds(7 + kw, quarter, stride=2), :].astype(BF16) for kh in range(3) for kw in range(3)
        ]
        result = silu(dot(jnp.concatenate(parts, axis=1), k2_ref[...])).astype(BF16).astype(F32)
        g_ref[w, 0] = result[:, :128]
        g_ref[w, 1] = result[:, 128:]
    count = quarter // 2
    finish_weight(0)
    tokens = None
    for w in range(2):
        for t in range(2):
            rows = jnp.concatenate([g_ref[w, k, pl.ds(t, count, stride=2), :] for k in range(2)], axis=1)
            part = we_ref[:, :, 2 * w + t].reshape(rows.shape[1], we_ref.shape[4])
            term = dot(rows.astype(BF16), part)
            tokens = term if tokens is None else tokens + term
    tok_ref[s] = tokens.astype(BF16)
    for way in range(2):

        @pl.when(has(1 - way, 1))
        def _(way=way):
            copy_tok(way, 0).start()

    pass_x(1)

    total_len = n * count
    lanes = lax.broadcasted_iota(jnp.int32, (count, total_len), 1)
    for d in range(1, n):
        copy_flag(d).wait_recv()

    def activity(k, row):
        block = order_ref[pl.ds(pl.multiple_of(k * count, count), count), :]
        return row + dot(flag_ref[k], jnp.where(lanes == block, 1.0, 0.0).astype(BF16))

    row = lax.fori_loop(0, n, activity, jnp.zeros((flag_ref.shape[1], total_len), F32))
    own = lanes == order_ref[pl.ds(pl.multiple_of(s * count, count), count), :]
    onehot = jnp.where(own, 1.0, 0.0).astype(BF16)
    bias = jnp.where((row[0:1, :] > 0.5) | own, 0.0, -jnp.inf)

    pass_y(1)
    relay(1)
    pass_x(2)
    pass_x(3)
    finish_weight(1)

    def place(k):
        normed = normalize(tok_ref[k])
        made = dot(normed, wp_ref[:, :, :, width:].reshape(width, 2 * width))
        kv_ref[pl.ds(pl.multiple_of(k * count, count), count), :] = made.astype(BF16)

    place(s)

    def place_both(k):
        for way in range(2):

            @pl.when(has(way, k))
            def _(way=way):
                place(s - k if way == 0 else s + k)

    def arrive(k, carry):
        relay(k)
        place_both(k)
        return carry

    if n > 1:
        place_both(1)
    pass_y(2)
    pass_y(3)
    lax.fori_loop(2, n, arrive, 0)
    mine = dot(onehot, tok_ref[...].reshape(total_len, width)).astype(BF16)
    head = width // HEADS
    finish_weight(2)
    query = dot(normalize(mine), wp_ref[:, :, :, :width].reshape(width, width))
    query = (query * head ** (-0.5)).astype(BF16)
    low_half = lax.broadcasted_iota(jnp.int32, (count, 2 * head), 1) < head
    bias = jnp.concatenate([bias, bias], axis=0)
    mixed = []
    for h in range(HEADS // 2):
        cols = slice(h * 2 * head, (h + 1) * 2 * head)
        pair = query[:, cols]
        zero = jnp.zeros_like(pair)
        both = jnp.concatenate([jnp.where(low_half, pair, zero), jnp.where(low_half, zero, pair)], axis=0)
        keys = kv_ref[:, cols]
        values = kv_ref[:, slice(width + h * 2 * head, width + (h + 1) * 2 * head)]
        scores = lax.dot_general(both, keys, (((1,), (1,)), ((), ())), preferred_element_type=F32) + bias
        weights = jnp.exp(scores - jnp.max(scores, axis=-1, keepdims=True))
        total = jnp.sum(weights, axis=-1, keepdims=True)
        result = dot(weights.astype(BF16), values) / total
        mixed.append(jnp.where(low_half, result[:count], result[count:]).astype(BF16))
    finish_weight(3)
    final = mine.astype(F32) + dot(jnp.concatenate(mixed, axis=1), wo_ref[...].reshape(width, width))
    out_ref[...] = final.astype(BF16)

    for w in range(4):
        copy_mate(w).wait_send()
        for d in steps:
            copy_x(w, d).wait_send()
            copy_y(w, d).wait_send()
            copy_fwd(w, d, 0).wait_send()
            copy_fwd(w, d, 1).wait_send()
    for d in range(1, n):
        copy_flag(d).wait_send()

    def drain(k, carry):
        for way in range(2):

            @pl.when(has(way, k) & has(1 - way, 1))
            def _(way=way):
                copy_tok(way, k).wait_send()

        return carry

    lax.fori_loop(0, n - 1, drain, 0)

    @pl.when(s < n - 1)
    def _():
        copy_halo(0).wait_send()
        copy_halo(1).wait_send()


def body(
    readout, first_kernel, second_kernel, embed_weight, project_weight, output_weight, order, active
):
    n, n_mp, n_sec = lax.axis_size("seq"), lax.axis_size("mp"), lax.axis_size("section")
    x = readout[0].transpose(1, 0, 2)
    wires, c_in, ticks = x.shape
    c_mid, c_out = second_kernel.shape[2:]
    width = embed_weight.shape[1]
    rows_e = embed_weight.shape[0] // 4
    embed = embed_weight.reshape(rows_e, 4, width).transpose(1, 0, 2)
    rows_p = project_weight.shape[0]
    count = active.shape[1]
    k2 = second_kernel.reshape(9 * c_mid, c_out)
    vmem = pl.BlockSpec(memory_space=pltpu.VMEM)
    hbm = pl.BlockSpec(memory_space=pl.ANY)
    dma = pltpu.SemaphoreType.DMA
    links = (4, n_mp - 1)
    result = pl.pallas_call(
        functools.partial(kernel, (n, n_mp)),
        out_shape=jax.ShapeDtypeStruct((count, width), BF16),
        in_specs=[vmem] * 5 + [hbm] * 3,
        out_specs=vmem,
        scratch_shapes=[
            pltpu.VMEM((n_mp, n_sec, 4, rows_e, width), BF16),
            pltpu.VMEM((n_mp, n_sec, rows_p, 3 * width), BF16),
            pltpu.VMEM((n_mp, n_sec, rows_p, width), BF16),
            pltpu.VMEM((c_in, ticks), BF16),
            pltpu.VMEM((ticks // 2, c_mid), BF16),
            pltpu.VMEM((ticks // 2, c_mid), BF16),
            pltpu.VMEM((ticks + 16, c_mid), F32),
            pltpu.VMEM((ticks + 16, c_mid), F32),
            pltpu.VMEM((ticks + 16, c_mid), F32),
            pltpu.VMEM((wires // 2 + 1, ticks // 2 + 16, c_mid), F32),
            pltpu.VMEM((wires // 4, 2, ticks // 4, c_out // 2), F32),
            pltpu.VMEM((n, count, width), BF16),
            pltpu.VMEM((n * count, 2 * width), BF16),
            pltpu.VMEM((n, 16, count), BF16),
            dma((4,)), dma((4,)), dma((4,)), dma(links), dma(links), dma(links), dma(links),
            dma(links + (2,)), dma(links + (2,)), dma((2,)), dma((2,)),
            dma((2, n)), dma((2, n)), dma((n - 1,)), dma((n - 1,)),
        ],
        compiler_params=pltpu.CompilerParams(
            collective_id=0, has_side_effects=True, vmem_limit_bytes=52 * 2**20
        ),
    )(x, first_kernel, k2, order[0][:, None], active, embed, project_weight, output_weight)
    return result[None]


def solution(mesh):
    in_specs = (
        P(("groups", "mp", "section"), None, "seq", None),
        P(),
        P(),
        P(("mp", "section"), None),
        P(("mp", "section"), None),
        P(("mp", "section"), None),
        P(("groups", "mp", "section"), None),
        P(("groups", "mp", "section"), "seq"),
    )
    out_specs = P(("groups", "mp", "section"), "seq", None)
    return jax.shard_map(body, mesh=mesh, in_specs=in_specs, out_specs=out_specs, check_vma=False)
```

```python
import functools

import jax
import jax.numpy as jnp
from jax import lax
from jax.experimental import pallas as pl
from jax.experimental.pallas import tpu as pltpu
from jax.sharding import PartitionSpec as P

HEADS = 12
epsilon = 1e-05
MESH = pl.DeviceIdType.MESH
F32 = jnp.float32
BF16 = jnp.bfloat16


def silu(v):
    return v / (1.0 + jnp.exp(-v))


def normalize(tokens):
    values = tokens.astype(F32)
    center = jnp.mean(values, axis=-1, keepdims=True)
    spread = jnp.mean(jnp.square(values - center), axis=-1, keepdims=True)
    return ((values - center) * lax.rsqrt(spread + epsilon)).astype(BF16)


def dot(a, b):
    return jnp.dot(a, b, preferred_element_type=F32)


def kernel(
    sizes,
    x_ref, k1_ref, k2_ref, order_ref, active_ref, embed_ref, project_ref, output_ref,
    out_ref,
    we_ref, wp_ref, wo_ref, hx_ref, h1_ref, s1_ref, p0_ref, p1_ref, p2_ref, f_ref, g_ref,
    tok_ref, kv_ref, flag_ref,
    local_sem, mate_send, mate_recv, x_send, x_recv, y_send, y_recv,
    fwd_send, fwd_recv, halo_send, halo_recv, tok_send, tok_recv, flag_send, flag_recv,
):
    n, n_mp = sizes
    g, s = lax.axis_index("groups"), lax.axis_index("seq")
    m, c = lax.axis_index("mp"), lax.axis_index("section")
    mate = {"section": 1 - c}
    across = {"groups": 1 - g}

    def mp_peer(d):
        return {"mp": lax.rem(m + d, n_mp)}

    def seq_peer(d):
        return {"seq": lax.rem(s + d, n)}

    def remote(src, dst, send, recv, where):
        return pltpu.make_async_remote_copy(
            src_ref=src, dst_ref=dst, send_sem=send, recv_sem=recv, device_id=where, device_id_type=MESH
        )

    barrier = pltpu.get_barrier_semaphore()
    peers = [mate, across] + [mp_peer(d) for d in range(1, n_mp)] + [seq_peer(d) for d in range(1, n)]
    for where in peers:
        pl.semaphore_signal(barrier, inc=1, device_id=where, device_id_type=MESH)
    pl.semaphore_wait(barrier, len(peers))

    width = wo_ref.shape[3]
    shards = (embed_ref, project_ref, project_ref, output_ref)
    full = (we_ref, wp_ref, wp_ref, wo_ref)
    spans = (None, (width, 2 * width), (0, width), (0, width))

    def half(ref, w, which):
        if w == 0:
            return ref.at[pl.ds(2 * which, 2)]
        base, cols = spans[w][0], spans[w][1] // 2
        return ref.at[:, pl.ds(pl.multiple_of(base + which * cols, 128), cols)]

    def span(ref, w):
        return ref if w == 0 else ref.at[:, pl.ds(*spans[w])]

    def copy_local(w):
        return pltpu.make_async_copy(span(shards[w], w), span(full[w].at[m, c], w), local_sem.at[w])

    def copy_mate(w):
        return remote(span(shards[w], w), span(full[w].at[m, c], w), mate_send.at[w], mate_recv.at[w], mate)

    def copy_x(w, d):
        return remote(
            half(shards[w], w, g), half(full[w].at[m, c], w, g), x_send.at[w, d - 1], x_recv.at[w, d - 1], mp_peer(d)
        )

    def piece(w, d, which):
        return half(full[w].at[lax.rem(m + n_mp - d, n_mp), c], w, which)

    def copy_y(w, d):
        ref = piece(w, d, g)
        return remote(ref, ref, y_send.at[w, d - 1], y_recv.at[w, d - 1], across)

    def copy_fwd(w, d, k):
        ref = piece(w, d, g if k == 0 else 1 - g)
        return remote(ref, ref, fwd_send.at[w, d - 1, k], fwd_recv.at[w, d - 1, k], mate)

    steps = range(1, n_mp)

    def send_weight(w):
        for d in steps:
            copy_x(w, d).start()
        copy_mate(w).start()
        copy_local(w).start()

    def pass_x(w):
        for d in steps:
            copy_x(w, d).wait_recv()
            copy_y(w, d).start()
            copy_fwd(w, d, 0).start()

    def pass_y(w):
        for d in steps:
            copy_y(w, d).wait_recv()
            copy_fwd(w, d, 1).start()

    def finish_weight(w):
        copy_local(w).wait()
        copy_mate(w).wait_recv()
        for d in steps:
            copy_fwd(w, d, 0).wait_recv()
            copy_fwd(w, d, 1).wait_recv()

    def copy_halo(k):
        src, dst = ((x_ref.at[x_ref.shape[0] - 1], hx_ref), (s1_ref, h1_ref))[k]
        return remote(src, dst, halo_send.at[k], halo_recv.at[k], seq_peer(1))

    def start_halo(k):
        @pl.when(s < n - 1)
        def _():
            copy_halo(k).start()

    def await_halo(k, ref):
        @pl.when(s > 0)
        def _():
            copy_halo(k).wait_recv()

        @pl.when(s == 0)
        def _():
            ref[...] = jnp.zeros_like(ref)

    def copy_flag(d):
        ref = flag_ref.at[s]
        return remote(ref, ref, flag_send.at[d - 1], flag_recv.at[d - 1], seq_peer(d))

    def copy_tok(d):
        ref = tok_ref.at[s]
        return remote(ref, ref, tok_send.at[d - 1], tok_recv.at[d - 1], seq_peer(d))

    start_halo(0)
    send_weight(0)
    flag_ref[s] = jnp.broadcast_to(active_ref[...].astype(F32), flag_ref.shape[1:]).astype(BF16)
    for d in range(1, n):
        copy_flag(d).start()

    ticks = x_ref.shape[2]
    half_ticks, quarter = ticks // 2, ticks // 4
    for ref in (p0_ref, p1_ref, p2_ref):
        ref[0:8, :] = jnp.zeros((8, ref.shape[1]), F32)
    rows1 = x_ref.shape[0] // 2
    for w in range(rows1 + 1):
        f_ref[w, 0:8, :] = jnp.zeros((8, f_ref.shape[2]), F32)
    c_in, c_mid = k1_ref.shape[2], k1_ref.shape[3]
    k1 = jnp.concatenate([k1_ref[:, kw].reshape(3 * c_in, c_mid) for kw in range(3)], axis=1)

    def conv_one(w):
        low = hx_ref[...] if w == 0 else x_ref[2 * w - 1]
        rows = jnp.concatenate([low, x_ref[2 * w], x_ref[2 * w + 1]], axis=0)
        made = lax.dot_general(rows, k1, (((0,), (0,)), ((), ())), preferred_element_type=F32)
        for kw, ref in enumerate((p0_ref, p1_ref, p2_ref)):
            ref[8 : 8 + ticks, :] = made[:, kw * c_mid : (kw + 1) * c_mid]
        total = (
            p0_ref[pl.ds(7, half_ticks, stride=2), :]
            + p1_ref[pl.ds(8, half_ticks, stride=2), :]
            + p2_ref[pl.ds(9, half_ticks, stride=2), :]
        )
        result = silu(total).astype(BF16)
        f_ref[w + 1, 8 : 8 + half_ticks, :] = result.astype(F32)
        return result

    s1_ref[...] = conv_one(rows1 - 1)
    start_halo(1)
    send_weight(1)
    send_weight(2)
    for w in range(1, rows1 - 1):
        conv_one(w)
    pass_x(0)
    await_halo(0, hx_ref)
    conv_one(0)
    send_weight(3)
    await_halo(1, h1_ref)
    f_ref[0, 8 : 8 + half_ticks, :] = h1_ref[...].astype(F32)
    pass_y(0)

    for w in range(rows1 // 2):
        parts = [
            f_ref[2 * w + kh, pl.ds(7 + kw, quarter, stride=2), :].astype(BF16) for kh in range(3) for kw in range(3)
        ]
        result = silu(dot(jnp.concatenate(parts, axis=1), k2_ref[...])).astype(BF16).astype(F32)
        g_ref[w, 0] = result[:, :128]
        g_ref[w, 1] = result[:, 128:]
    count = quarter // 2
    finish_weight(0)
    tokens = None
    for w in range(2):
        for t in range(2):
            rows = jnp.concatenate([g_ref[w, k, pl.ds(t, count, stride=2), :] for k in range(2)], axis=1)
            part = we_ref[:, :, 2 * w + t].reshape(rows.shape[1], we_ref.shape[4])
            term = dot(rows.astype(BF16), part)
            tokens = term if tokens is None else tokens + term
    tok_ref[s] = tokens.astype(BF16)
    for d in range(1, n):
        copy_tok(d).start()
    pass_x(1)

    total_len = n * count
    lanes = lax.broadcasted_iota(jnp.int32, (count, total_len), 1)
    for d in range(1, n):
        copy_flag(d).wait_recv()

    def activity(k, row):
        block = order_ref[pl.ds(pl.multiple_of(k * count, count), count), :]
        return row + dot(flag_ref[k], jnp.where(lanes == block, 1.0, 0.0).astype(BF16))

    row = lax.fori_loop(0, n, activity, jnp.zeros((flag_ref.shape[1], total_len), F32))
    own = lanes == order_ref[pl.ds(pl.multiple_of(s * count, count), count), :]
    onehot = jnp.where(own, 1.0, 0.0).astype(BF16)
    bias = jnp.where((row[0:1, :] > 0.5) | own, 0.0, -jnp.inf)

    pass_x(2)
    pass_y(1)
    pass_x(3)
    finish_weight(1)

    def place(k):
        normed = normalize(tok_ref[k])
        made = dot(normed, wp_ref[:, :, :, width:].reshape(width, 2 * width))
        kv_ref[pl.ds(pl.multiple_of(k * count, count), count), :] = made.astype(BF16)

    place(s)

    pass_y(2)
    pass_y(3)

    def arrive(d, carry):
        copy_tok(d).wait_recv()
        place(lax.rem(s + n - d, n))
        return carry

    lax.fori_loop(1, n, arrive, 0)
    mine = dot(onehot, tok_ref[...].reshape(total_len, width)).astype(BF16)
    head = width // HEADS
    finish_weight(2)
    query = dot(normalize(mine), wp_ref[:, :, :, :width].reshape(width, width))
    query = (query * head ** (-0.5)).astype(BF16)
    low_half = lax.broadcasted_iota(jnp.int32, (count, 2 * head), 1) < head
    bias = jnp.concatenate([bias, bias], axis=0)
    mixed = []
    for h in range(HEADS // 2):
        cols = slice(h * 2 * head, (h + 1) * 2 * head)
        pair = query[:, cols]
        zero = jnp.zeros_like(pair)
        both = jnp.concatenate([jnp.where(low_half, pair, zero), jnp.where(low_half, zero, pair)], axis=0)
        keys = kv_ref[:, cols]
        values = kv_ref[:, slice(width + h * 2 * head, width + (h + 1) * 2 * head)]
        scores = lax.dot_general(both, keys, (((1,), (1,)), ((), ())), preferred_element_type=F32) + bias
        weights = jnp.exp(scores - jnp.max(scores, axis=-1, keepdims=True))
        total = jnp.sum(weights, axis=-1, keepdims=True)
        result = dot(weights.astype(BF16), values) / total
        mixed.append(jnp.where(low_half, result[:count], result[count:]).astype(BF16))
    finish_weight(3)
    final = mine.astype(F32) + dot(jnp.concatenate(mixed, axis=1), wo_ref[...].reshape(width, width))
    out_ref[...] = final.astype(BF16)

    for w in range(4):
        copy_mate(w).wait_send()
        for d in steps:
            copy_x(w, d).wait_send()
            copy_y(w, d).wait_send()
            copy_fwd(w, d, 0).wait_send()
            copy_fwd(w, d, 1).wait_send()
    for d in range(1, n):
        copy_flag(d).wait_send()
        copy_tok(d).wait_send()

    @pl.when(s < n - 1)
    def _():
        copy_halo(0).wait_send()
        copy_halo(1).wait_send()


def body(
    readout, first_kernel, second_kernel, embed_weight, project_weight, output_weight, order, active
):
    n, n_mp, n_sec = lax.axis_size("seq"), lax.axis_size("mp"), lax.axis_size("section")
    x = readout[0].transpose(1, 0, 2)
    wires, c_in, ticks = x.shape
    c_mid, c_out = second_kernel.shape[2:]
    width = embed_weight.shape[1]
    rows_e = embed_weight.shape[0] // 4
    embed = embed_weight.reshape(rows_e, 4, width).transpose(1, 0, 2)
    rows_p = project_weight.shape[0]
    count = active.shape[1]
    k2 = second_kernel.reshape(9 * c_mid, c_out)
    vmem = pl.BlockSpec(memory_space=pltpu.VMEM)
    hbm = pl.BlockSpec(memory_space=pl.ANY)
    dma = pltpu.SemaphoreType.DMA
    links = (4, n_mp - 1)
    result = pl.pallas_call(
        functools.partial(kernel, (n, n_mp)),
        out_shape=jax.ShapeDtypeStruct((count, width), BF16),
        in_specs=[vmem] * 5 + [hbm] * 3,
        out_specs=vmem,
        scratch_shapes=[
            pltpu.VMEM((n_mp, n_sec, 4, rows_e, width), BF16),
            pltpu.VMEM((n_mp, n_sec, rows_p, 3 * width), BF16),
            pltpu.VMEM((n_mp, n_sec, rows_p, width), BF16),
            pltpu.VMEM((c_in, ticks), BF16),
            pltpu.VMEM((ticks // 2, c_mid), BF16),
            pltpu.VMEM((ticks // 2, c_mid), BF16),
            pltpu.VMEM((ticks + 16, c_mid), F32),
            pltpu.VMEM((ticks + 16, c_mid), F32),
            pltpu.VMEM((ticks + 16, c_mid), F32),
            pltpu.VMEM((wires // 2 + 1, ticks // 2 + 16, c_mid), F32),
            pltpu.VMEM((wires // 4, 2, ticks // 4, c_out // 2), F32),
            pltpu.VMEM((n, count, width), BF16),
            pltpu.VMEM((n * count, 2 * width), BF16),
            pltpu.VMEM((n, 16, count), BF16),
            dma((4,)), dma((4,)), dma((4,)), dma(links), dma(links), dma(links), dma(links),
            dma(links + (2,)), dma(links + (2,)), dma((2,)), dma((2,)),
            dma((n - 1,)), dma((n - 1,)), dma((n - 1,)), dma((n - 1,)),
        ],
        compiler_params=pltpu.CompilerParams(
            collective_id=0, has_side_effects=True, vmem_limit_bytes=52 * 2**20
        ),
    )(x, first_kernel, k2, order[0][:, None], active, embed, project_weight, output_weight)
    return result[None]


def solution(mesh):
    in_specs = (
        P(("groups", "mp", "section"), None, "seq", None),
        P(),
        P(),
        P(("mp", "section"), None),
        P(("mp", "section"), None),
        P(("mp", "section"), None),
        P(("groups", "mp", "section"), None),
        P(("groups", "mp", "section"), "seq"),
    )
    out_specs = P(("groups", "mp", "section"), "seq", None)
    return jax.shard_map(body, mesh=mesh, in_specs=in_specs, out_specs=out_specs, check_vma=False)
```

```python
import functools

import jax
import jax.numpy as jnp
from jax import lax
from jax.experimental import pallas as pl
from jax.experimental.pallas import tpu as pltpu
from jax.sharding import PartitionSpec as P

HEADS = 12
epsilon = 1e-05
MESH = pl.DeviceIdType.MESH
F32 = jnp.float32
BF16 = jnp.bfloat16


def silu(v):
    return v / (1.0 + jnp.exp(-v))


def normalize(tokens):
    values = tokens.astype(F32)
    center = jnp.mean(values, axis=-1, keepdims=True)
    spread = jnp.mean(jnp.square(values - center), axis=-1, keepdims=True)
    return ((values - center) * lax.rsqrt(spread + epsilon)).astype(BF16)


def dot(a, b):
    return jnp.dot(a, b, preferred_element_type=F32)


def kernel(
    sizes,
    raw_ref, k1_ref, k2_ref, order_ref, active_ref, embed_ref, project_ref, output_ref,
    out_ref,
    we_ref, wp_ref, wo_ref, hx_ref, h1_ref, s1_ref, p0_ref, p1_ref, p2_ref, f_ref, g_ref,
    tok_ref, kv_ref, flag_ref, x_ref, split_ref, act_ref, act_sem,
    local_sem, mate_send, mate_recv, x_send, x_recv, y_send, y_recv,
    fwd_send, fwd_recv, halo_send, halo_recv, tok_send, tok_recv, flag_send, flag_recv,
):
    n, n_mp = sizes
    g, s = lax.axis_index("groups"), lax.axis_index("seq")
    m, c = lax.axis_index("mp"), lax.axis_index("section")
    mate = {"section": 1 - c}
    across = {"groups": 1 - g}

    def mp_peer(d):
        return {"mp": lax.rem(m + d, n_mp)}

    def seq_peer(d):
        return {"seq": lax.rem(s + d, n)}

    def remote(src, dst, send, recv, where):
        return pltpu.make_async_remote_copy(
            src_ref=src, dst_ref=dst, send_sem=send, recv_sem=recv, device_id=where, device_id_type=MESH
        )

    copy_act = pltpu.make_async_copy(active_ref, act_ref, act_sem)
    copy_act.start()
    barrier = pltpu.get_barrier_semaphore()
    peers = [mate, across] + [mp_peer(d) for d in range(1, n_mp)] + [seq_peer(d) for d in range(1, n)]
    for where in peers:
        pl.semaphore_signal(barrier, inc=1, device_id=where, device_id_type=MESH)
    pl.semaphore_wait(barrier, len(peers))

    width = wo_ref.shape[3]
    shards = (embed_ref, project_ref, project_ref, output_ref)
    full = (we_ref, wp_ref, wp_ref, wo_ref)
    spans = (None, (width, 2 * width), (0, width), (0, width))

    def half(ref, w, which):
        if w == 0:
            return ref.at[pl.ds(2 * which, 2)]
        base, cols = spans[w][0], spans[w][1] // 2
        return ref.at[:, pl.ds(pl.multiple_of(base + which * cols, 128), cols)]

    def span(ref, w):
        return ref if w == 0 else ref.at[:, pl.ds(*spans[w])]

    def copy_local(w):
        return pltpu.make_async_copy(span(shards[w], w), span(full[w].at[m, c], w), local_sem.at[w])

    def copy_mate(w):
        return remote(span(shards[w], w), span(full[w].at[m, c], w), mate_send.at[w], mate_recv.at[w], mate)

    def copy_x(w, d):
        return remote(
            half(shards[w], w, g), half(full[w].at[m, c], w, g), x_send.at[w, d - 1], x_recv.at[w, d - 1], mp_peer(d)
        )

    def piece(w, d, which):
        return half(full[w].at[lax.rem(m + n_mp - d, n_mp), c], w, which)

    def copy_y(w, d):
        ref = piece(w, d, g)
        return remote(ref, ref, y_send.at[w, d - 1], y_recv.at[w, d - 1], across)

    def copy_fwd(w, d, k):
        ref = piece(w, d, g if k == 0 else 1 - g)
        return remote(ref, ref, fwd_send.at[w, d - 1, k], fwd_recv.at[w, d - 1, k], mate)

    steps = range(1, n_mp)

    def send_weight(w):
        for d in steps:
            copy_x(w, d).start()
        copy_mate(w).start()
        copy_local(w).start()

    def pass_x(w):
        for d in steps:
            copy_x(w, d).wait_recv()
            copy_y(w, d).start()
            copy_fwd(w, d, 0).start()

    def pass_y(w):
        for d in steps:
            copy_y(w, d).wait_recv()
            copy_fwd(w, d, 1).start()

    def finish_weight(w):
        copy_local(w).wait()
        copy_mate(w).wait_recv()
        for d in steps:
            copy_fwd(w, d, 0).wait_recv()
            copy_fwd(w, d, 1).wait_recv()

    def copy_halo(k):
        src, dst = ((x_ref.at[x_ref.shape[0] - 1], hx_ref), (s1_ref, h1_ref))[k]
        return remote(src, dst, halo_send.at[k], halo_recv.at[k], seq_peer(1))

    def start_halo(k):
        @pl.when(s < n - 1)
        def _():
            copy_halo(k).start()

    def await_halo(k, ref):
        @pl.when(s > 0)
        def _():
            copy_halo(k).wait_recv()

        @pl.when(s == 0)
        def _():
            ref[...] = jnp.zeros_like(ref)

    def copy_flag(d):
        ref = flag_ref.at[s]
        return remote(ref, ref, flag_send.at[d - 1], flag_recv.at[d - 1], seq_peer(d))

    def copy_tok(d):
        ref = tok_ref.at[s]
        return remote(ref, ref, tok_send.at[d - 1], tok_recv.at[d - 1], seq_peer(d))

    send_weight(0)
    c_rows, wires = raw_ref.shape[0], raw_ref.shape[1]
    blocks = raw_ref.shape[2] // 128
    for b in range(blocks):
        part = raw_ref[:, :, b * 128 : (b + 1) * 128].astype(F32)
        split_ref[b] = part.reshape(c_rows * wires, 128)
    for w in reversed(range(wires)):
        cells = [split_ref[b, pl.ds(w, c_rows, stride=wires), :] for b in range(blocks)]
        x_ref[w] = jnp.concatenate(cells, axis=1).astype(BF16)
        if w == wires - 1:
            start_halo(0)
    copy_act.wait()
    flag_ref[s] = jnp.broadcast_to(act_ref[...].astype(F32), flag_ref.shape[1:]).astype(BF16)
    for d in range(1, n):
        copy_flag(d).start()

    ticks = x_ref.shape[2]
    half_ticks, quarter = ticks // 2, ticks // 4
    for ref in (p0_ref, p1_ref, p2_ref):
        ref[0:8, :] = jnp.zeros((8, ref.shape[1]), F32)
    rows1 = x_ref.shape[0] // 2
    for w in range(rows1 + 1):
        f_ref[w, 0:8, :] = jnp.zeros((8, f_ref.shape[2]), F32)
    c_in, c_mid = k1_ref.shape[2], k1_ref.shape[3]
    k1 = jnp.concatenate([k1_ref[:, kw].reshape(3 * c_in, c_mid) for kw in range(3)], axis=1)

    def conv_one(w):
        low = hx_ref[...] if w == 0 else x_ref[2 * w - 1]
        rows = jnp.concatenate([low, x_ref[2 * w], x_ref[2 * w + 1]], axis=0)
        made = lax.dot_general(rows, k1, (((0,), (0,)), ((), ())), preferred_element_type=F32)
        for kw, ref in enumerate((p0_ref, p1_ref, p2_ref)):
            ref[8 : 8 + ticks, :] = made[:, kw * c_mid : (kw + 1) * c_mid]
        total = (
            p0_ref[pl.ds(7, half_ticks, stride=2), :]
            + p1_ref[pl.ds(8, half_ticks, stride=2), :]
            + p2_ref[pl.ds(9, half_ticks, stride=2), :]
        )
        result = silu(total).astype(BF16)
        f_ref[w + 1, 8 : 8 + half_ticks, :] = result.astype(F32)
        return result

    s1_ref[...] = conv_one(rows1 - 1)
    start_halo(1)
    send_weight(1)
    send_weight(2)
    for w in range(1, rows1 - 1):
        conv_one(w)
    pass_x(0)
    await_halo(0, hx_ref)
    conv_one(0)
    send_weight(3)
    await_halo(1, h1_ref)
    f_ref[0, 8 : 8 + half_ticks, :] = h1_ref[...].astype(F32)
    pass_y(0)

    for w in range(rows1 // 2):
        parts = [
            f_ref[2 * w + kh, pl.ds(7 + kw, quarter, stride=2), :].astype(BF16) for kh in range(3) for kw in range(3)
        ]
        result = silu(dot(jnp.concatenate(parts, axis=1), k2_ref[...])).astype(BF16).astype(F32)
        g_ref[w, 0] = result[:, :128]
        g_ref[w, 1] = result[:, 128:]
    count = quarter // 2
    finish_weight(0)
    tokens = None
    for w in range(2):
        for t in range(2):
            rows = jnp.concatenate([g_ref[w, k, pl.ds(t, count, stride=2), :] for k in range(2)], axis=1)
            part = we_ref[:, :, 2 * w + t].reshape(rows.shape[1], we_ref.shape[4])
            term = dot(rows.astype(BF16), part)
            tokens = term if tokens is None else tokens + term
    tok_ref[s] = tokens.astype(BF16)
    for d in range(1, n):
        copy_tok(d).start()
    pass_x(1)

    total_len = n * count
    lanes = lax.broadcasted_iota(jnp.int32, (count, total_len), 1)
    for d in range(1, n):
        copy_flag(d).wait_recv()

    def order_column(k):
        spread = jnp.broadcast_to(order_ref[pl.ds(k, 1), :].astype(F32), (count, count))
        return jnp.transpose(spread)[:, 0:1].astype(jnp.int32)

    def activity(k, row):
        block = order_column(k)
        return row + dot(flag_ref[k], jnp.where(lanes == block, 1.0, 0.0).astype(BF16))

    row = lax.fori_loop(0, n, activity, jnp.zeros((flag_ref.shape[1], total_len), F32))
    own = lanes == order_column(s)
    onehot = jnp.where(own, 1.0, 0.0).astype(BF16)
    bias = jnp.where((row[0:1, :] > 0.5) | own, 0.0, -jnp.inf)

    pass_x(2)
    pass_y(1)
    pass_x(3)
    finish_weight(1)

    def place(k):
        normed = normalize(tok_ref[k])
        made = dot(normed, wp_ref[:, :, :, width:].reshape(width, 2 * width))
        kv_ref[pl.ds(pl.multiple_of(k * count, count), count), :] = made.astype(BF16)

    place(s)

    pass_y(2)
    pass_y(3)

    def arrive(d, carry):
        copy_tok(d).wait_recv()
        place(lax.rem(s + n - d, n))
        return carry

    lax.fori_loop(1, n, arrive, 0)
    mine = dot(onehot, tok_ref[...].reshape(total_len, width)).astype(BF16)
    head = width // HEADS
    finish_weight(2)
    query = dot(normalize(mine), wp_ref[:, :, :, :width].reshape(width, width))
    query = (query * head ** (-0.5)).astype(BF16)
    low_half = lax.broadcasted_iota(jnp.int32, (count, 2 * head), 1) < head
    bias = jnp.concatenate([bias, bias], axis=0)
    mixed = []
    for h in range(HEADS // 2):
        cols = slice(h * 2 * head, (h + 1) * 2 * head)
        pair = query[:, cols]
        zero = jnp.zeros_like(pair)
        both = jnp.concatenate([jnp.where(low_half, pair, zero), jnp.where(low_half, zero, pair)], axis=0)
        keys = kv_ref[:, cols]
        values = kv_ref[:, slice(width + h * 2 * head, width + (h + 1) * 2 * head)]
        scores = lax.dot_general(both, keys, (((1,), (1,)), ((), ())), preferred_element_type=F32) + bias
        weights = jnp.exp(scores - jnp.max(scores, axis=-1, keepdims=True))
        total = jnp.sum(weights, axis=-1, keepdims=True)
        result = dot(weights.astype(BF16), values) / total
        mixed.append(jnp.where(low_half, result[:count], result[count:]).astype(BF16))
    finish_weight(3)
    final = mine.astype(F32) + dot(jnp.concatenate(mixed, axis=1), wo_ref[...].reshape(width, width))
    out_ref[...] = final.astype(BF16)

    for w in range(4):
        copy_mate(w).wait_send()
        for d in steps:
            copy_x(w, d).wait_send()
            copy_y(w, d).wait_send()
            copy_fwd(w, d, 0).wait_send()
            copy_fwd(w, d, 1).wait_send()
    for d in range(1, n):
        copy_flag(d).wait_send()
        copy_tok(d).wait_send()

    @pl.when(s < n - 1)
    def _():
        copy_halo(0).wait_send()
        copy_halo(1).wait_send()


def body(
    readout, first_kernel, second_kernel, embed_weight, project_weight, output_weight, order, active
):
    n, n_mp, n_sec = lax.axis_size("seq"), lax.axis_size("mp"), lax.axis_size("section")
    x = readout[0]
    c_in, wires, ticks = x.shape
    c_mid, c_out = second_kernel.shape[2:]
    width = embed_weight.shape[1]
    rows_e = embed_weight.shape[0] // 4
    embed = embed_weight.reshape(rows_e, 4, width).transpose(1, 0, 2)
    rows_p = project_weight.shape[0]
    count = active.shape[1]
    k2 = second_kernel.reshape(9 * c_mid, c_out)
    vmem = pl.BlockSpec(memory_space=pltpu.VMEM)
    hbm = pl.BlockSpec(memory_space=pl.ANY)
    dma = pltpu.SemaphoreType.DMA
    links = (4, n_mp - 1)
    result = pl.pallas_call(
        functools.partial(kernel, (n, n_mp)),
        out_shape=jax.ShapeDtypeStruct((count, width), BF16),
        in_specs=[vmem] * 4 + [hbm] * 4,
        out_specs=vmem,
        scratch_shapes=[
            pltpu.VMEM((n_mp, n_sec, 4, rows_e, width), BF16),
            pltpu.VMEM((n_mp, n_sec, rows_p, 3 * width), BF16),
            pltpu.VMEM((n_mp, n_sec, rows_p, width), BF16),
            pltpu.VMEM((c_in, ticks), BF16),
            pltpu.VMEM((ticks // 2, c_mid), BF16),
            pltpu.VMEM((ticks // 2, c_mid), BF16),
            pltpu.VMEM((ticks + 16, c_mid), F32),
            pltpu.VMEM((ticks + 16, c_mid), F32),
            pltpu.VMEM((ticks + 16, c_mid), F32),
            pltpu.VMEM((wires // 2 + 1, ticks // 2 + 16, c_mid), F32),
            pltpu.VMEM((wires // 4, 2, ticks // 4, c_out // 2), F32),
            pltpu.VMEM((n, count, width), BF16),
            pltpu.VMEM((n * count, 2 * width), BF16),
            pltpu.VMEM((n, 16, count), BF16),
            pltpu.VMEM((wires, c_in, ticks), BF16),
            pltpu.VMEM((ticks // 128, c_in * wires, 128), F32),
            pltpu.VMEM((1, count), jnp.int32),
            dma,
            dma((4,)), dma((4,)), dma((4,)), dma(links), dma(links), dma(links), dma(links),
            dma(links + (2,)), dma(links + (2,)), dma((2,)), dma((2,)),
            dma((n - 1,)), dma((n - 1,)), dma((n - 1,)), dma((n - 1,)),
        ],
        compiler_params=pltpu.CompilerParams(
            collective_id=0, has_side_effects=True, vmem_limit_bytes=52 * 2**20
        ),
    )(x, first_kernel, k2, order.reshape(n, count), active, embed, project_weight, output_weight)
    return result[None]


def solution(mesh):
    in_specs = (
        P(("groups", "mp", "section"), None, "seq", None),
        P(),
        P(),
        P(("mp", "section"), None),
        P(("mp", "section"), None),
        P(("mp", "section"), None),
        P(("groups", "mp", "section"), None),
        P(("groups", "mp", "section"), "seq"),
    )
    out_specs = P(("groups", "mp", "section"), "seq", None)
    return jax.shard_map(body, mesh=mesh, in_specs=in_specs, out_specs=out_specs, check_vma=False)
```

```python
import functools

import jax
import jax.numpy as jnp
from jax import lax
from jax.experimental import pallas as pl
from jax.experimental.pallas import tpu as pltpu
from jax.sharding import PartitionSpec as P

HEADS = 12
epsilon = 1e-05
MESH = pl.DeviceIdType.MESH
F32 = jnp.float32
BF16 = jnp.bfloat16


def silu(v):
    return v / (1.0 + jnp.exp(-v))


def normalize(tokens):
    values = tokens.astype(F32)
    center = jnp.mean(values, axis=-1, keepdims=True)
    spread = jnp.mean(jnp.square(values - center), axis=-1, keepdims=True)
    return ((values - center) * lax.rsqrt(spread + epsilon)).astype(BF16)


def dot(a, b):
    return jnp.dot(a, b, preferred_element_type=F32)


def kernel(
    sizes,
    raw_ref, k1_ref, k2_ref, order_ref, active_ref, embed_ref, project_ref, output_ref,
    out_ref,
    we_ref, wp_ref, wo_ref, hx_ref, h1_ref, s1_ref, p0_ref, p1_ref, p2_ref, f_ref, g_ref,
    tok_ref, kv_ref, flag_ref, x_ref, split_ref, act_ref, act_sem,
    local_sem, mate_send, mate_recv, x_send, x_recv, y_send, y_recv,
    fwd_send, fwd_recv, halo_send, halo_recv, tok_send, tok_recv, flag_send, flag_recv,
):
    n, n_mp = sizes
    g, s = lax.axis_index("groups"), lax.axis_index("seq")
    m, c = lax.axis_index("mp"), lax.axis_index("section")
    mate = {"section": 1 - c}
    across = {"groups": 1 - g}

    def mp_peer(d):
        return {"mp": lax.rem(m + d, n_mp)}

    def seq_peer(d):
        return {"seq": lax.rem(s + d, n)}

    def remote(src, dst, send, recv, where):
        return pltpu.make_async_remote_copy(
            src_ref=src, dst_ref=dst, send_sem=send, recv_sem=recv, device_id=where, device_id_type=MESH
        )

    copy_act = pltpu.make_async_copy(active_ref, act_ref, act_sem)
    copy_act.start()
    barrier = pltpu.get_barrier_semaphore()
    peers = [mate, across] + [mp_peer(d) for d in range(1, n_mp)] + [seq_peer(d) for d in range(1, n)]
    for where in peers:
        pl.semaphore_signal(barrier, inc=1, device_id=where, device_id_type=MESH)
    pl.semaphore_wait(barrier, len(peers))

    width = wo_ref.shape[3]
    shards = (embed_ref, project_ref, project_ref, output_ref)
    full = (we_ref, wp_ref, wp_ref, wo_ref)
    spans = (None, (width, 2 * width), (0, width), (0, width))

    def half(ref, w, which):
        if w == 0:
            return ref.at[pl.ds(2 * which, 2)]
        base, cols = spans[w][0], spans[w][1] // 2
        return ref.at[:, pl.ds(pl.multiple_of(base + which * cols, 128), cols)]

    def span(ref, w):
        return ref if w == 0 else ref.at[:, pl.ds(*spans[w])]

    def copy_local(w):
        return pltpu.make_async_copy(span(shards[w], w), span(full[w].at[m, c], w), local_sem.at[w])

    def copy_mate(w):
        return remote(span(shards[w], w), span(full[w].at[m, c], w), mate_send.at[w], mate_recv.at[w], mate)

    def copy_x(w, d):
        return remote(
            half(shards[w], w, g), half(full[w].at[m, c], w, g), x_send.at[w, d - 1], x_recv.at[w, d - 1], mp_peer(d)
        )

    def piece(w, d, which):
        return half(full[w].at[lax.rem(m + n_mp - d, n_mp), c], w, which)

    def copy_y(w, d):
        ref = piece(w, d, g)
        return remote(ref, ref, y_send.at[w, d - 1], y_recv.at[w, d - 1], across)

    def copy_fwd(w, d, k):
        ref = piece(w, d, g if k == 0 else 1 - g)
        return remote(ref, ref, fwd_send.at[w, d - 1, k], fwd_recv.at[w, d - 1, k], mate)

    steps = range(1, n_mp)

    def send_weight(w):
        for d in steps:
            copy_x(w, d).start()
        copy_mate(w).start()
        copy_local(w).start()

    def pass_x(w):
        for d in steps:
            copy_x(w, d).wait_recv()
            copy_y(w, d).start()
            copy_fwd(w, d, 0).start()

    def pass_y(w):
        for d in steps:
            copy_y(w, d).wait_recv()
            copy_fwd(w, d, 1).start()

    def finish_weight(w):
        copy_local(w).wait()
        copy_mate(w).wait_recv()
        for d in steps:
            copy_fwd(w, d, 0).wait_recv()
            copy_fwd(w, d, 1).wait_recv()

    def copy_halo(k):
        src, dst = ((x_ref.at[x_ref.shape[0] - 1], hx_ref), (s1_ref, h1_ref))[k]
        return remote(src, dst, halo_send.at[k], halo_recv.at[k], seq_peer(1))

    def start_halo(k):
        @pl.when(s < n - 1)
        def _():
            copy_halo(k).start()

    def await_halo(k, ref):
        @pl.when(s > 0)
        def _():
            copy_halo(k).wait_recv()

        @pl.when(s == 0)
        def _():
            ref[...] = jnp.zeros_like(ref)

    def copy_flag(d):
        ref = flag_ref.at[s]
        return remote(ref, ref, flag_send.at[d - 1], flag_recv.at[d - 1], seq_peer(d))

    def copy_tok(d):
        ref = tok_ref.at[s]
        return remote(ref, ref, tok_send.at[d - 1], tok_recv.at[d - 1], seq_peer(d))

    send_weight(0)
    c_rows, wires = raw_ref.shape[0], raw_ref.shape[1]
    blocks = raw_ref.shape[2] // 128
    for b in range(blocks):
        part = raw_ref[:, :, b * 128 : (b + 1) * 128].astype(F32)
        split_ref[b] = part.reshape(c_rows * wires, 128)
    for w in reversed(range(wires)):
        cells = [split_ref[b, pl.ds(w, c_rows, stride=wires), :] for b in range(blocks)]
        x_ref[w] = jnp.concatenate(cells, axis=1).astype(BF16)
        if w == wires - 1:
            start_halo(0)
    copy_act.wait()
    flag_ref[s] = jnp.broadcast_to(act_ref[...].astype(F32), flag_ref.shape[1:]).astype(BF16)
    for d in range(1, n):
        copy_flag(d).start()

    ticks = x_ref.shape[2]
    half_ticks, quarter = ticks // 2, ticks // 4
    for ref in (p0_ref, p1_ref, p2_ref):
        ref[0:8, :] = jnp.zeros((8, ref.shape[1]), F32)
    rows1 = x_ref.shape[0] // 2
    for w in range(rows1 + 1):
        f_ref[w, 0:8, :] = jnp.zeros((8, f_ref.shape[2]), F32)
    c_in, c_mid = k1_ref.shape[2], k1_ref.shape[3]
    k1 = jnp.concatenate([k1_ref[:, kw].reshape(3 * c_in, c_mid) for kw in range(3)], axis=1)

    def conv_one(w):
        low = hx_ref[...] if w == 0 else x_ref[2 * w - 1]
        rows = jnp.concatenate([low, x_ref[2 * w], x_ref[2 * w + 1]], axis=0)
        made = lax.dot_general(rows, k1, (((0,), (0,)), ((), ())), preferred_element_type=F32)
        for kw, ref in enumerate((p0_ref, p1_ref, p2_ref)):
            ref[8 : 8 + ticks, :] = made[:, kw * c_mid : (kw + 1) * c_mid]
        total = (
            p0_ref[pl.ds(7, half_ticks, stride=2), :]
            + p1_ref[pl.ds(8, half_ticks, stride=2), :]
            + p2_ref[pl.ds(9, half_ticks, stride=2), :]
        )
        result = silu(total).astype(BF16)
        f_ref[w + 1, 8 : 8 + half_ticks, :] = result.astype(F32)
        return result

    s1_ref[...] = conv_one(rows1 - 1)
    start_halo(1)
    send_weight(1)
    send_weight(2)
    for w in range(1, rows1 - 1):
        conv_one(w)
    pass_x(0)
    await_halo(0, hx_ref)
    conv_one(0)
    send_weight(3)
    await_halo(1, h1_ref)
    f_ref[0, 8 : 8 + half_ticks, :] = h1_ref[...].astype(F32)
    pass_y(0)

    for w in range(rows1 // 2):
        parts = [
            f_ref[2 * w + kh, pl.ds(7 + kw, quarter, stride=2), :].astype(BF16) for kh in range(3) for kw in range(3)
        ]
        result = silu(dot(jnp.concatenate(parts, axis=1), k2_ref[...])).astype(BF16).astype(F32)
        g_ref[w, 0] = result[:, :128]
        g_ref[w, 1] = result[:, 128:]
    count = quarter // 2
    finish_weight(0)
    tokens = None
    for w in range(2):
        for t in range(2):
            rows = jnp.concatenate([g_ref[w, k, pl.ds(t, count, stride=2), :] for k in range(2)], axis=1)
            part = we_ref[:, :, 2 * w + t].reshape(rows.shape[1], we_ref.shape[4])
            term = dot(rows.astype(BF16), part)
            tokens = term if tokens is None else tokens + term
    tok_ref[s] = tokens.astype(BF16)
    for d in range(1, n):
        copy_tok(d).start()
    pass_x(1)

    total_len = n * count
    lanes = lax.broadcasted_iota(jnp.int32, (count, total_len), 1)
    for d in range(1, n):
        copy_flag(d).wait_recv()

    def order_column(k):
        spread = jnp.broadcast_to(order_ref[pl.ds(k, 1), :].astype(F32), (count, count))
        return jnp.transpose(spread)[:, 0:1].astype(jnp.int32)

    def activity(k, row):
        block = order_column(k)
        return row + dot(flag_ref[k], jnp.where(lanes == block, 1.0, 0.0).astype(BF16))

    row = lax.fori_loop(0, n, activity, jnp.zeros((flag_ref.shape[1], total_len), F32))
    own = lanes == order_column(s)
    onehot = jnp.where(own, 1.0, 0.0).astype(BF16)
    bias = jnp.where((row[0:1, :] > 0.5) | own, 0.0, -jnp.inf)

    pass_x(2)
    pass_y(1)
    pass_x(3)
    finish_weight(1)

    def place(k):
        normed = normalize(tok_ref[k])
        made = dot(normed, wp_ref[:, :, :, width:].reshape(width, 2 * width))
        kv_ref[pl.ds(pl.multiple_of(k * count, count), count), :] = made.astype(BF16)

    place(s)

    pass_y(2)
    pass_y(3)

    def arrive(step, carry):
        d = lax.select(2 * s < n, n - step, step)
        copy_tok(d).wait_recv()
        place(lax.rem(s + n - d, n))
        return carry

    lax.fori_loop(1, n, arrive, 0)
    mine = dot(onehot, tok_ref[...].reshape(total_len, width)).astype(BF16)
    head = width // HEADS
    finish_weight(2)
    query = dot(normalize(mine), wp_ref[:, :, :, :width].reshape(width, width))
    query = (query * head ** (-0.5)).astype(BF16)
    low_half = lax.broadcasted_iota(jnp.int32, (count, 2 * head), 1) < head
    bias = jnp.concatenate([bias, bias], axis=0)
    mixed = []
    for h in range(HEADS // 2):
        cols = slice(h * 2 * head, (h + 1) * 2 * head)
        pair = query[:, cols]
        zero = jnp.zeros_like(pair)
        both = jnp.concatenate([jnp.where(low_half, pair, zero), jnp.where(low_half, zero, pair)], axis=0)
        keys = kv_ref[:, cols]
        values = kv_ref[:, slice(width + h * 2 * head, width + (h + 1) * 2 * head)]
        scores = lax.dot_general(both, keys, (((1,), (1,)), ((), ())), preferred_element_type=F32) + bias
        weights = jnp.exp(scores - jnp.max(scores, axis=-1, keepdims=True))
        total = jnp.sum(weights, axis=-1, keepdims=True)
        result = dot(weights.astype(BF16), values) / total
        mixed.append(jnp.where(low_half, result[:count], result[count:]).astype(BF16))
    finish_weight(3)
    final = mine.astype(F32) + dot(jnp.concatenate(mixed, axis=1), wo_ref[...].reshape(width, width))
    out_ref[...] = final.astype(BF16)

    for w in range(4):
        copy_mate(w).wait_send()
        for d in steps:
            copy_x(w, d).wait_send()
            copy_y(w, d).wait_send()
            copy_fwd(w, d, 0).wait_send()
            copy_fwd(w, d, 1).wait_send()
    for d in range(1, n):
        copy_flag(d).wait_send()
        copy_tok(d).wait_send()

    @pl.when(s < n - 1)
    def _():
        copy_halo(0).wait_send()
        copy_halo(1).wait_send()


def body(
    readout, first_kernel, second_kernel, embed_weight, project_weight, output_weight, order, active
):
    n, n_mp, n_sec = lax.axis_size("seq"), lax.axis_size("mp"), lax.axis_size("section")
    x = readout[0]
    c_in, wires, ticks = x.shape
    c_mid, c_out = second_kernel.shape[2:]
    width = embed_weight.shape[1]
    rows_e = embed_weight.shape[0] // 4
    embed = embed_weight.reshape(rows_e, 4, width).transpose(1, 0, 2)
    rows_p = project_weight.shape[0]
    count = active.shape[1]
    k2 = second_kernel.reshape(9 * c_mid, c_out)
    vmem = pl.BlockSpec(memory_space=pltpu.VMEM)
    hbm = pl.BlockSpec(memory_space=pl.ANY)
    dma = pltpu.SemaphoreType.DMA
    links = (4, n_mp - 1)
    result = pl.pallas_call(
        functools.partial(kernel, (n, n_mp)),
        out_shape=jax.ShapeDtypeStruct((count, width), BF16),
        in_specs=[vmem] * 4 + [hbm] * 4,
        out_specs=vmem,
        scratch_shapes=[
            pltpu.VMEM((n_mp, n_sec, 4, rows_e, width), BF16),
            pltpu.VMEM((n_mp, n_sec, rows_p, 3 * width), BF16),
            pltpu.VMEM((n_mp, n_sec, rows_p, width), BF16),
            pltpu.VMEM((c_in, ticks), BF16),
            pltpu.VMEM((ticks // 2, c_mid), BF16),
            pltpu.VMEM((ticks // 2, c_mid), BF16),
            pltpu.VMEM((ticks + 16, c_mid), F32),
            pltpu.VMEM((ticks + 16, c_mid), F32),
            pltpu.VMEM((ticks + 16, c_mid), F32),
            pltpu.VMEM((wires // 2 + 1, ticks // 2 + 16, c_mid), F32),
            pltpu.VMEM((wires // 4, 2, ticks // 4, c_out // 2), F32),
            pltpu.VMEM((n, count, width), BF16),
            pltpu.VMEM((n * count, 2 * width), BF16),
            pltpu.VMEM((n, 16, count), BF16),
            pltpu.VMEM((wires, c_in, ticks), BF16),
            pltpu.VMEM((ticks // 128, c_in * wires, 128), F32),
            pltpu.VMEM((1, count), jnp.int32),
            dma,
            dma((4,)), dma((4,)), dma((4,)), dma(links), dma(links), dma(links), dma(links),
            dma(links + (2,)), dma(links + (2,)), dma((2,)), dma((2,)),
            dma((n - 1,)), dma((n - 1,)), dma((n - 1,)), dma((n - 1,)),
        ],
        compiler_params=pltpu.CompilerParams(
            collective_id=0, has_side_effects=True, vmem_limit_bytes=52 * 2**20
        ),
    )(x, first_kernel, k2, order.reshape(n, count), active, embed, project_weight, output_weight)
    return result[None]


def solution(mesh):
    in_specs = (
        P(("groups", "mp", "section"), None, "seq", None),
        P(),
        P(),
        P(("mp", "section"), None),
        P(("mp", "section"), None),
        P(("mp", "section"), None),
        P(("groups", "mp", "section"), None),
        P(("groups", "mp", "section"), "seq"),
    )
    out_specs = P(("groups", "mp", "section"), "seq", None)
    return jax.shard_map(body, mesh=mesh, in_specs=in_specs, out_specs=out_specs, check_vma=False)
```
